512 devices in a mesh: wide: 32 (over z, core), sub: 16 (over x, y).
Axes of the slice: x: 4, y: 4, z: 16, core: 2. Of those that a mesh axis runs over, the one named last changes fastest.
Arguments:
- passages: bfloat16 [256, 1024], P('sub'), may hold values from -6 to 6
- enc_weight: bfloat16 [1024, 262144], P(None, ('wide', 'sub')), may hold values from -0.1875 to 0.1875
- enc_bias: float32 [262144], P(('wide', 'sub')), may hold values from -4 to 4
- dec_weight: bfloat16 [262144, 1024], P(('wide', 'sub')), may hold values from -0.0234375 to 0.0234375
- dec_bias: float32 [1024], replicated, may hold values from -4 to 4
- active: int32 [256, 262144], P(None, ('wide', 'sub')), may hold values 0 or 1
Outputs:
- grad_enc: bfloat16 [1024, 262144], P(None, ('wide', 'sub'))
- grad_enc_bias: float32 [262144], P(('wide', 'sub'))
- grad_dec: bfloat16 [262144, 1024], P(('wide', 'sub'))
- grad_dec_bias: float32 [1024], replicated
- grad_input: float32 [256, 1024], P('sub')
The draws below stay inside these ranges and needn't reach their ends.
All inputs are finite; a program needn't handle non-finite values. No bound on the sum of `active` on one device may be relied on, other than what follows from the above.
Results may differ from the reference program's by a relative error of at most 0.014.
Values may be sent and summed in bfloat16 or wider, within the bound.
A program may use at most 64 MiB of HBM per device.

```python
import jax
import jax.numpy as jnp

D = 1024
LATENTS = 262144
ROWS = 256


def plant(values, rng, least, largest):
    shape = values.shape
    spot = [jax.random.randint(jax.random.fold_in(rng, axis), (), 0, shape[axis]) for axis in range(len(shape))]
    values = values.at[tuple(spot)].set(least)
    longest = shape.index(max(shape))
    spot[longest] = (spot[longest] + 1) % shape[longest]
    return values.at[tuple(spot)].set(largest)


def block_scale(key, dims, cuts, low, largest):
    def one(dim, shards_of):
        steps = jax.random.uniform(jax.random.fold_in(jax.random.fold_in(key, 6), dim), (shards_of,), jnp.float32, low / len(cuts), largest / len(cuts))
        return jnp.repeat(jnp.exp(steps), dims[dim] // shards_of).reshape((-1,) + (1,) * (len(dims) - dim - 1))

    level = one(*cuts[0])
    for cut in cuts[1:]:
        level = level * one(*cut)
    return level


def noise(own_key, shape, spread, reach, shards=(), held_as=jnp.bfloat16):
    array = spread * jax.random.normal(own_key, shape, jnp.float32)
    if shards:
        array = array * block_scale(own_key, shape, shards, -0.22, 0.18)
    return jnp.clip(array, -reach, reach).astype(held_as)


def setup_inputs(seed: int = 0) -> dict:
    streams_of = jax.random.split(jax.random.key(seed), 7)
    return {
        "passages": noise(streams_of[0], (ROWS, D), 1.0, 6.0, ((0, 16),)),
        "enc_weight": noise(streams_of[1], (D, LATENTS), D ** -0.5, 0.1875, ((1, 512),)),
        "enc_bias": noise(streams_of[2], (LATENTS,), 0.7, 4.0, ((0, 512),), jnp.float32),
        "dec_weight": noise(streams_of[3], (LATENTS, D), (LATENTS // 4) ** -0.5, 0.0234375, ((0, 512),)),
        "dec_bias": noise(streams_of[4], (D,), 0.7, 4.0, (), jnp.float32),
        "active": plant((jax.random.randint(streams_of[5], (ROWS, LATENTS), 0, 4) < 1).astype(jnp.int32), jax.random.fold_in(streams_of[5], 1), 0, 1),
    }


def reference(passages, enc_weight, enc_bias, dec_weight, dec_bias, active):
    gate = active.astype(jnp.float32)
    pre = jnp.dot(passages, enc_weight, preferred_element_type=jnp.float32) + enc_bias
    codes = (gate * pre).astype(jnp.bfloat16)
    recon = jnp.dot(codes, dec_weight, preferred_element_type=jnp.float32) + dec_bias
    resid = (recon - passages.astype(jnp.float32)).astype(jnp.bfloat16)
    grad_dec = jnp.dot(codes.T, resid, preferred_element_type=jnp.float32).astype(jnp.bfloat16)
    grad_dec_bias = jnp.sum(resid.astype(jnp.float32), axis=0)
    back = jnp.dot(resid, dec_weight.T, preferred_element_type=jnp.float32)
    dpre = (gate * back).astype(jnp.bfloat16)
    grad_enc = jnp.dot(passages.T, dpre, preferred_element_type=jnp.float32).astype(jnp.bfloat16)
    grad_enc_bias = jnp.sum(dpre.astype(jnp.float32), axis=0)
    grad_input = jnp.dot(dpre, enc_weight.T, preferred_element_type=jnp.float32) - resid.astype(jnp.float32)
    return grad_enc, grad_enc_bias, grad_dec, grad_dec_bias, grad_input
```

```python
import functools

import jax
import jax.numpy as jnp
from jax import lax
from jax.experimental import pallas as pl
from jax.experimental.pallas import tpu as pltpu
from jax.sharding import PartitionSpec as P

MESH = pl.DeviceIdType.MESH
BF16 = jnp.bfloat16
F32 = jnp.float32
ROWS, D, LAT = 256, 1024, 512
OWN, HALF, QUARTER = 16, 512, 256
SIDE, DEPTH = 4, 16


def ring(d, n):
    return min(d, n - d)


def dot_nt(a, b):
    return lax.dot_general(a, b, (((1,), (1,)), ((), ())), preferred_element_type=F32)


def dot_nn(a, b):
    return jnp.dot(a, b, preferred_element_type=F32)


def kernel(
    pas_in, enc_in, eb, dec_in, db, act_in,
    genc_out, geb_out, gdec_out, gdb_out, gin_out,
    enc, dec, act, every, every_t, pre, codes, codes_t, resid, dpre,
    swap_out, swap_in, parts, rows_in, rows_z, gdec, genc, final,
    load_sem, store_sem, send_sem, recv_sem, swap_send, swap_recv,
):
    wide, sub = lax.axis_index("wide"), lax.axis_index("sub")
    z, c = wide // 2, wide % 2
    x, y = sub // SIDE, sub % SIDE
    zp = z % 2
    zn = z + 1 - 2 * zp
    oc = 1 - c
    mine = pl.ds(pl.multiple_of(sub * OWN, OWN), OWN)

    sub_offsets = sorted(
        ((dx, dy) for dx in range(SIDE) for dy in range(SIDE)),
        key=lambda o: -ring(o[0], SIDE) - ring(o[1], SIDE),
    )
    subs = [((x + dx) % SIDE) * SIDE + (y + dy) % SIDE for dx, dy in sub_offsets]
    others = subs[:-1]
    sibling = (z * 2 + oc, sub)
    z_peers = [
        (((z + d) % DEPTH) * 2 + c, sub)
        for d in sorted(range(1, DEPTH), key=lambda d: -ring(d, DEPTH))
    ]

    loads = [
        pltpu.make_async_copy(
            pas_in.at[:, pl.ds(pl.multiple_of(c * HALF, HALF), HALF)],
            every.at[c, mine],
            load_sem.at[0],
        ),
        pltpu.make_async_copy(enc_in, enc, load_sem.at[1]),
        pltpu.make_async_copy(act_in, act, load_sem.at[2]),
        pltpu.make_async_copy(dec_in, dec, load_sem.at[3]),
    ]
    for load in loads:
        load.start()

    barrier = pltpu.get_barrier_semaphore()
    greeted = [(wide, s) for s in others] + [(zn * 2 + c, s) for s in others]
    greeted += z_peers + [sibling]
    for peer in greeted:
        pl.semaphore_signal(barrier, inc=1, device_id=peer, device_id_type=MESH)
    loads[0].wait()
    pl.semaphore_wait(barrier, len(greeted))

    def send(src, dst, k, peer):
        pltpu.make_async_remote_copy(
            src_ref=src, dst_ref=dst, send_sem=send_sem.at[k], recv_sem=recv_sem.at[k],
            device_id=peer, device_id_type=MESH,
        ).start()

    def arrived(ref, k):
        pltpu.make_async_copy(ref, ref, recv_sem.at[k]).wait()

    def sent(ref, k):
        pltpu.make_async_copy(ref, ref, send_sem.at[k]).wait()

    def swap(src, dst, k):
        copy = pltpu.make_async_remote_copy(
            src_ref=src, dst_ref=dst, send_sem=swap_send.at[k], recv_sem=swap_recv.at[k],
            device_id=sibling, device_id_type=MESH,
        )
        copy.start()
        return copy

    def gather(array, k, swap_k):
        for s in others:
            send(array.at[c, mine], array.at[c, mine], k, (wide, s))
        rest = array.at[c, pl.ds(0, ROWS - OWN)]
        arrived(rest, k)
        return swap(array.at[c], array.at[c], swap_k), rest

    def half(h):
        return pl.ds(pl.multiple_of(h * HALF, HALF), HALF)

    def quarter(q):
        return pl.ds(pl.multiple_of(q * QUARTER, QUARTER), QUARTER)

    def reduce_out(i, part):
        swaps = []
        for t in range(2):
            zq = zp if t else 1 - zp
            swap_out[i, t] = part(oc * 2 + zq).astype(BF16)
            swaps.append(swap(swap_out.at[i, t], swap_in.at[i, t], 2 + 2 * i + t))
        slot = zp * 16 + sub
        k = 2 + 2 * i
        for t in range(2):
            zq = zp if t else 1 - zp
            own = part(c * 2 + zq)
            swaps[t].wait_recv()
            parts[i, t] = (own + swap_in[i, t].astype(F32)).astype(BF16)
            for s in others if t else subs:
                rows = pl.ds(pl.multiple_of(s * OWN, OWN), OWN)
                peer = (wide if t else zn * 2 + c, s)
                send(parts.at[i, t, rows], rows_in.at[i, slot], k, peer)
        rows_in[i, slot] = parts[i, 1, mine]
        return swaps

    def pieces_along_z(i):
        k = 2 + 2 * i
        arrived(rows_in.at[i, pl.ds(0, 31)], k)
        total = rows_in[i, 0].astype(F32)
        for n in range(1, 32):
            total = total + rows_in[i, n].astype(F32)
        rows_z[i, z] = total.astype(BF16)
        for peer in z_peers:
            send(rows_z.at[i, z], rows_z.at[i, z], k + 1, peer)

    def sum_along_z(i, zq):
        total = rows_z[i, zq].astype(F32)
        for n in range(1, DEPTH // 2):
            total = total + rows_z[i, 2 * n + zq].astype(F32)
        return total

    def reduce_sent(i, swaps):
        for copy in swaps:
            copy.wait_send()
        sent(rows_in.at[i, pl.ds(0, 31)], 2 + 2 * i)
        sent(rows_z.at[i, pl.ds(0, 15)], 3 + 2 * i)

    passages_swap, passages_rest = gather(every, 0, 0)
    loads[1].wait()
    pre[...] = dot_nn(every[c], enc[half(c), :])
    loads[2].wait()
    loads[3].wait()
    passages_swap.wait_recv()
    both = pre[...] + dot_nn(every[oc], enc[half(oc), :]) + eb[...]
    codes[...] = (act[...].astype(F32) * both).astype(BF16)

    swaps_0 = reduce_out(0, lambda q: dot_nn(codes[...], dec[:, quarter(q)]))
    codes_t[...] = codes[...].T
    pieces_along_z(0)
    every_t[0] = every[0].T
    every_t[1] = every[1].T
    arrived(rows_z.at[0, pl.ds(0, 15)], 3)
    for zq in range(2):
        recon = sum_along_z(0, zq) + db[:, quarter(c * 2 + zq)]
        columns = pl.ds(zq * QUARTER, QUARTER)
        resid[c, mine, columns] = (recon - every[c, mine, columns].astype(F32)).astype(BF16)
    resid_swap, resid_rest = gather(resid, 1, 1)
    pre[...] = dot_nt(resid[c], dec[:, half(c)])
    resid_swap.wait_recv()
    back = pre[...] + dot_nt(resid[oc], dec[:, half(oc)])
    dpre[...] = (act[...].astype(F32) * back).astype(BF16)

    swaps_1 = reduce_out(1, lambda q: dot_nt(dpre[...], enc[quarter(q), :]))
    stores = []
    for h in range(2):
        gdec[:, pl.ds(h * HALF, HALF)] = dot_nn(codes_t[...], resid[h]).astype(BF16)
        gdb_out[:, pl.ds(h * HALF, HALF)] = jnp.sum(resid[h].astype(F32), axis=0, keepdims=True)
    stores.append(pltpu.make_async_copy(gdec, gdec_out, store_sem.at[0]))
    stores[0].start()
    for h in range(2):
        genc[pl.ds(h * HALF, HALF), :] = dot_nn(every_t[h], dpre[...]).astype(BF16)
    stores.append(pltpu.make_async_copy(genc, genc_out, store_sem.at[1]))
    stores[1].start()
    geb_out[...] = jnp.sum(dpre[...].astype(F32), axis=0, keepdims=True)
    pieces_along_z(1)
    passages_swap.wait_send()
    resid_swap.wait_send()
    sent(passages_rest, 0)
    sent(resid_rest, 1)
    reduce_sent(0, swaps_0)
    arrived(rows_z.at[1, pl.ds(0, 15)], 5)
    for zq in range(2):
        final[c, :, pl.ds(zq * QUARTER, QUARTER)] = sum_along_z(1, zq)
    final_swap = swap(final.at[c], final.at[c], 6)
    reduce_sent(1, swaps_1)
    for store in stores:
        store.wait()
    final_swap.wait()
    for h in range(2):
        gin_out[:, pl.ds(h * HALF, HALF)] = final[h] - resid[h, mine].astype(F32)


def per_device(passages, enc_weight, enc_bias, dec_weight, dec_bias, active):
    anywhere = pl.BlockSpec(memory_space=pl.ANY)
    vmem = pl.BlockSpec(memory_space=pltpu.VMEM)
    genc, geb, gdec, gdb, gin = pl.pallas_call(
        kernel,
        out_shape=(
            jax.ShapeDtypeStruct((D, LAT), BF16),
            jax.ShapeDtypeStruct((1, LAT), F32),
            jax.ShapeDtypeStruct((LAT, D), BF16),
            jax.ShapeDtypeStruct((1, D), F32),
            jax.ShapeDtypeStruct((OWN, D), F32),
        ),
        in_specs=[anywhere, anywhere, vmem, anywhere, vmem, anywhere],
        out_specs=(anywhere, vmem, anywhere, vmem, vmem),
        scratch_shapes=[
            pltpu.VMEM((D, LAT), BF16),
            pltpu.VMEM((LAT, D), BF16),
            pltpu.VMEM((ROWS, LAT), jnp.int32),
            pltpu.VMEM((2, ROWS, HALF), BF16),
            pltpu.VMEM((2, HALF, ROWS), BF16),
            pltpu.VMEM((ROWS, LAT), F32),
            pltpu.VMEM((ROWS, LAT), BF16),
            pltpu.VMEM((LAT, ROWS), BF16),
            pltpu.VMEM((2, ROWS, HALF), BF16),
            pltpu.VMEM((ROWS, LAT), BF16),
            pltpu.VMEM((2, 2, ROWS, QUARTER), BF16),
            pltpu.VMEM((2, 2, ROWS, QUARTER), BF16),
            pltpu.VMEM((2, 2, ROWS, QUARTER), BF16),
            pltpu.VMEM((2, 32, OWN, QUARTER), BF16),
            pltpu.VMEM((2, DEPTH, OWN, QUARTER), BF16),
            pltpu.VMEM((LAT, D), BF16),
            pltpu.VMEM((D, LAT), BF16),
            pltpu.VMEM((2, OWN, HALF), F32),
            pltpu.SemaphoreType.DMA((4,)),
            pltpu.SemaphoreType.DMA((2,)),
            pltpu.SemaphoreType.DMA((6,)),
            pltpu.SemaphoreType.DMA((6,)),
            pltpu.SemaphoreType.DMA((7,)),
            pltpu.SemaphoreType.DMA((7,)),
        ],
        compiler_params=pltpu.CompilerParams(
            collective_id=0, has_side_effects=True, vmem_limit_bytes=40 * 2**20
        ),
        cost_estimate=pl.CostEstimate(
            flops=10 * ROWS * D * LAT, bytes_accessed=5 * 2**20, transcendentals=0
        ),
        name="sae_backward",
    )(passages, enc_weight, enc_bias.reshape(1, LAT), dec_weight, dec_bias.reshape(1, D), active)
    return genc, geb.reshape(LAT), gdec, gdb.reshape(D), gin


def solution(mesh):
    split = P(None, ("wide", "sub"))
    rows = P(("wide", "sub"), None)
    line = P(("wide", "sub"))
    return jax.shard_map(
        per_device,
        mesh=mesh,
        in_specs=(P("sub", None), split, line, rows, P(), split),
        out_specs=(split, line, rows, P(), P("sub", None)),
        check_vma=False,
    )
```

```python
import functools

import jax
import jax.numpy as jnp
from jax import lax
from jax.experimental import pallas as pl
from jax.experimental.pallas import tpu as pltpu
from jax.sharding import PartitionSpec as P

MESH = pl.DeviceIdType.MESH
BF16 = jnp.bfloat16
F32 = jnp.float32
ROWS, D, LAT = 256, 1024, 512
OWN, HALF, QUARTER = 16, 512, 256
SIDE, DEPTH = 4, 16


def ring(d, n):
    return min(d, n - d)


def dot_nt(a, b):
    return lax.dot_general(a, b, (((1,), (1,)), ((), ())), preferred_element_type=F32)


def dot_nn(a, b):
    return jnp.dot(a, b, preferred_element_type=F32)


def kernel(
    pas_in, enc_in, eb_in, dec_in, db_in, act_in,
    genc_out, geb_out, gdec_out, gdb_out, gin_out,
    enc, dec, act, eb, db, every, every_t, pre, codes, codes_t, resid, dpre,
    swap_out, swap_in, parts, rows_in, rows_z, gdec, genc, final,
    load_sem, store_sem, send_sem, recv_sem, swap_send, swap_recv,
):
    wide, sub = lax.axis_index("wide"), lax.axis_index("sub")
    z, c = wide // 2, wide % 2
    x, y = sub // SIDE, sub % SIDE
    zp = z % 2
    zn = z + 1 - 2 * zp
    oc = 1 - c
    mine = pl.ds(pl.multiple_of(sub * OWN, OWN), OWN)

    sub_offsets = sorted(
        ((dx, dy) for dx in range(SIDE) for dy in range(SIDE)),
        key=lambda o: -ring(o[0], SIDE) - ring(o[1], SIDE),
    )
    subs = [((x + dx) % SIDE) * SIDE + (y + dy) % SIDE for dx, dy in sub_offsets]
    others = subs[:-1]
    sibling = (z * 2 + oc, sub)
    z_peers = [
        (((z + d) % DEPTH) * 2 + c, sub)
        for d in sorted(range(1, DEPTH), key=lambda d: -ring(d, DEPTH))
    ]

    loads = [
        pltpu.make_async_copy(
            pas_in.at[:, pl.ds(pl.multiple_of(c * HALF, HALF), HALF)],
            every.at[c, mine],
            load_sem.at[0],
        ),
        pltpu.make_async_copy(enc_in, enc, load_sem.at[1]),
        pltpu.make_async_copy(act_in, act, load_sem.at[2]),
        pltpu.make_async_copy(eb_in, eb, load_sem.at[3]),
        pltpu.make_async_copy(dec_in, dec, load_sem.at[4]),
        pltpu.make_async_copy(db_in, db, load_sem.at[5]),
    ]
    for load in loads:
        load.start()

    barrier = pltpu.get_barrier_semaphore()
    greeted = [(wide, s) for s in others] + [(zn * 2 + c, s) for s in others]
    greeted += z_peers + [sibling]
    for peer in greeted:
        pl.semaphore_signal(barrier, inc=1, device_id=peer, device_id_type=MESH)
    loads[0].wait()
    pl.semaphore_wait(barrier, len(greeted))

    pending = []

    def send(src, dst, k, peer):
        pltpu.make_async_remote_copy(
            src_ref=src, dst_ref=dst, send_sem=send_sem.at[k], recv_sem=recv_sem.at[k],
            device_id=peer, device_id_type=MESH,
        ).start()

    def arrived(ref, k):
        pltpu.make_async_copy(ref, ref, recv_sem.at[k]).wait()

    def sent(ref, k):
        pltpu.make_async_copy(ref, ref, send_sem.at[k]).wait()

    def swap(src, dst, k):
        copy = pltpu.make_async_remote_copy(
            src_ref=src, dst_ref=dst, send_sem=swap_send.at[k], recv_sem=swap_recv.at[k],
            device_id=sibling, device_id_type=MESH,
        )
        copy.start()
        pending.append(copy.wait_send)
        return copy

    def gather(array, k, swap_k):
        for s in others:
            send(array.at[c, mine], array.at[c, mine], k, (wide, s))
        rest = array.at[c, pl.ds(0, ROWS - OWN)]
        pending.append(lambda: sent(rest, k))
        arrived(rest, k)
        return swap(array.at[c], array.at[c], swap_k)

    def half(h):
        return pl.ds(pl.multiple_of(h * HALF, HALF), HALF)

    def quarter(q):
        return pl.ds(pl.multiple_of(q * QUARTER, QUARTER), QUARTER)

    def reduce_out(i, part):
        swaps = []
        for t in range(2):
            zq = zp if t else 1 - zp
            swap_out[i, t] = part(oc * 2 + zq).astype(BF16)
            swaps.append(swap(swap_out.at[i, t], swap_in.at[i, t], 2 + 2 * i + t))
        slot = zp * 16 + sub
        k = 2 + 2 * i
        for t in range(2):
            zq = zp if t else 1 - zp
            own = part(c * 2 + zq)
            swaps[t].wait_recv()
            parts[i, t] = (own + swap_in[i, t].astype(F32)).astype(BF16)
            for s in others if t else subs:
                rows = pl.ds(pl.multiple_of(s * OWN, OWN), OWN)
                peer = (wide if t else zn * 2 + c, s)
                send(parts.at[i, t, rows], rows_in.at[i, slot], k, peer)
        rows_in[i, slot] = parts[i, 1, mine]
        pending.append(lambda: sent(rows_in.at[i, pl.ds(0, 31)], k))

    def pieces_along_z(i):
        k = 2 + 2 * i
        arrived(rows_in.at[i, pl.ds(0, 31)], k)
        total = rows_in[i, 0].astype(F32)
        for n in range(1, 32):
            total = total + rows_in[i, n].astype(F32)
        rows_z[i, z] = total.astype(BF16)
        for peer in z_peers:
            send(rows_z.at[i, z], rows_z.at[i, z], k + 1, peer)
        pending.append(lambda: sent(rows_z.at[i, pl.ds(0, 15)], k + 1))

    def sum_along_z(i, zq):
        total = rows_z[i, zq].astype(F32)
        for n in range(1, DEPTH // 2):
            total = total + rows_z[i, 2 * n + zq].astype(F32)
        return total

    passages_swap = gather(every, 0, 0)
    loads[1].wait()
    pre[...] = dot_nn(every[c], enc[half(c), :])
    for load in loads[2:]:
        load.wait()
    passages_swap.wait_recv()
    both = pre[...] + dot_nn(every[oc], enc[half(oc), :]) + eb[...]
    codes[...] = (act[...].astype(F32) * both).astype(BF16)

    reduce_out(0, lambda q: dot_nn(codes[...], dec[:, quarter(q)]))
    codes_t[...] = codes[...].T
    pieces_along_z(0)
    every_t[0] = every[0].T
    every_t[1] = every[1].T
    arrived(rows_z.at[0, pl.ds(0, 15)], 3)
    for zq in range(2):
        recon = sum_along_z(0, zq) + db[:, quarter(c * 2 + zq)]
        columns = pl.ds(zq * QUARTER, QUARTER)
        resid[c, mine, columns] = (recon - every[c, mine, columns].astype(F32)).astype(BF16)
    resid_swap = gather(resid, 1, 1)
    pre[...] = dot_nt(resid[c], dec[:, half(c)])
    resid_swap.wait_recv()
    back = pre[...] + dot_nt(resid[oc], dec[:, half(oc)])
    dpre[...] = (act[...].astype(F32) * back).astype(BF16)

    reduce_out(1, lambda q: dot_nt(dpre[...], enc[quarter(q), :]))
    for h in range(2):
        gdec[:, pl.ds(h * HALF, HALF)] = dot_nn(codes_t[...], resid[h]).astype(BF16)
        gdb_out[:, pl.ds(h * HALF, HALF)] = jnp.sum(resid[h].astype(F32), axis=0, keepdims=True)
    stores = [pltpu.make_async_copy(gdec, gdec_out, store_sem.at[0])]
    stores[0].start()
    pending.append(stores[0].wait)
    for h in range(2):
        genc[pl.ds(h * HALF, HALF), :] = dot_nn(every_t[h], dpre[...]).astype(BF16)
    stores.append(pltpu.make_async_copy(genc, genc_out, store_sem.at[1]))
    stores[1].start()
    pending.append(stores[1].wait)
    geb_out[...] = jnp.sum(dpre[...].astype(F32), axis=0, keepdims=True)
    pieces_along_z(1)
    arrived(rows_z.at[1, pl.ds(0, 15)], 5)
    for zq in range(2):
        final[c, :, pl.ds(zq * QUARTER, QUARTER)] = sum_along_z(1, zq)
    final_swap = swap(final.at[c], final.at[c], 6)
    final_swap.wait_recv()
    for wait in pending:
        wait()
    for h in range(2):
        gin_out[:, pl.ds(h * HALF, HALF)] = final[h] - resid[h, mine].astype(F32)


def place(genc_in, geb_in, gdec_in, gdb_in, gin_in, genc, geb, gdec, gdb, gin, sem):
    pairs = [(genc_in, genc), (gdec_in, gdec), (gin_in, gin), (geb_in, geb), (gdb_in, gdb)]
    copies = [pltpu.make_async_copy(a, b, sem.at[i]) for i, (a, b) in enumerate(pairs)]
    for copy in copies:
        copy.start()
    for copy in copies:
        copy.wait()


def per_device(passages, enc_weight, enc_bias, dec_weight, dec_bias, active):
    anywhere = pl.BlockSpec(memory_space=pl.ANY)
    vmem = pl.BlockSpec(memory_space=pltpu.VMEM)
    shapes = (
        jax.ShapeDtypeStruct((D, LAT), BF16),
        jax.ShapeDtypeStruct((1, LAT), F32),
        jax.ShapeDtypeStruct((LAT, D), BF16),
        jax.ShapeDtypeStruct((1, D), F32),
        jax.ShapeDtypeStruct((OWN, D), F32),
    )
    results = pl.pallas_call(
        kernel,
        out_shape=shapes,
        in_specs=[pl.BlockSpec(memory_space=pltpu.HBM)] * 6,
        out_specs=(anywhere, vmem, anywhere, vmem, vmem),
        scratch_shapes=[
            pltpu.VMEM((D, LAT), BF16),
            pltpu.VMEM((LAT, D), BF16),
            pltpu.VMEM((ROWS, LAT), jnp.int32),
            pltpu.VMEM((1, LAT), F32),
            pltpu.VMEM((1, D), F32),
            pltpu.VMEM((2, ROWS, HALF), BF16),
            pltpu.VMEM((2, HALF, ROWS), BF16),
            pltpu.VMEM((ROWS, LAT), F32),
            pltpu.VMEM((ROWS, LAT), BF16),
            pltpu.VMEM((LAT, ROWS), BF16),
            pltpu.VMEM((2, ROWS, HALF), BF16),
            pltpu.VMEM((ROWS, LAT), BF16),
            pltpu.VMEM((2, 2, ROWS, QUARTER), BF16),
            pltpu.VMEM((2, 2, ROWS, QUARTER), BF16),
            pltpu.VMEM((2, 2, ROWS, QUARTER), BF16),
            pltpu.VMEM((2, 32, OWN, QUARTER), BF16),
            pltpu.VMEM((2, DEPTH, OWN, QUARTER), BF16),
            pltpu.VMEM((LAT, D), BF16),
            pltpu.VMEM((D, LAT), BF16),
            pltpu.VMEM((2, OWN, HALF), F32),
            pltpu.SemaphoreType.DMA((6,)),
            pltpu.SemaphoreType.DMA((2,)),
            pltpu.SemaphoreType.DMA((6,)),
            pltpu.SemaphoreType.DMA((6,)),
            pltpu.SemaphoreType.DMA((7,)),
            pltpu.SemaphoreType.DMA((7,)),
        ],
        compiler_params=pltpu.CompilerParams(
            collective_id=0, has_side_effects=True, vmem_limit_bytes=63 * 2**20
        ),
        cost_estimate=pl.CostEstimate(
            flops=10 * ROWS * D * LAT, bytes_accessed=5 * 2**20, transcendentals=0
        ),
        name="sae_backward",
    )(passages, enc_weight, enc_bias.reshape(1, LAT), dec_weight, dec_bias.reshape(1, D), active)
    genc, geb, gdec, gdb, gin = pl.pallas_call(
        place,
        out_shape=shapes,
        in_specs=[anywhere] * 5,
        out_specs=[anywhere] * 5,
        scratch_shapes=[pltpu.SemaphoreType.DMA((5,))],
        compiler_params=pltpu.CompilerParams(vmem_limit_bytes=63 * 2**20),
        name="place",
    )(*results)
    return genc, geb.reshape(LAT), gdec, gdb.reshape(D), gin


def solution(mesh):
    split = P(None, ("wide", "sub"))
    rows = P(("wide", "sub"), None)
    line = P(("wide", "sub"))
    return jax.shard_map(
        per_device,
        mesh=mesh,
        in_specs=(P("sub", None), split, line, rows, P(), split),
        out_specs=(split, line, rows, P(), P("sub", None)),
        check_vma=False,
    )
```

```python
import functools

import jax
import jax.numpy as jnp
from jax import lax
from jax.experimental import pallas as pl
from jax.experimental.pallas import tpu as pltpu
from jax.sharding import PartitionSpec as P

MESH = pl.DeviceIdType.MESH
BF16 = jnp.bfloat16
F32 = jnp.float32
ROWS, D, LAT = 256, 1024, 512
OWN, HALF, QUARTER = 16, 512, 256
SIDE, DEPTH = 4, 16


def ring(d, n):
    return min(d, n - d)


def dot_nt(a, b):
    return lax.dot_general(a, b, (((1,), (1,)), ((), ())), preferred_element_type=F32)


def dot_nn(a, b):
    return jnp.dot(a, b, preferred_element_type=F32)


def kernel(
    pas_in, enc_in, eb_in, dec_in, db_in, act_in,
    genc_out, geb_out, gdec_out, gdb_out, gin_out,
    enc, dec, act, eb, db, every, every_t, pre, codes, codes_t, resid, dpre,
    swap_out, swap_in, parts, rows_in, rows_z, final,
    load_sem, send_sem, recv_sem, swap_send, swap_recv,
):
    wide, sub = lax.axis_index("wide"), lax.axis_index("sub")
    z, c = wide // 2, wide % 2
    x, y = sub // SIDE, sub % SIDE
    zp = z % 2
    zn = z + 1 - 2 * zp
    oc = 1 - c
    mine = pl.ds(pl.multiple_of(sub * OWN, OWN), OWN)

    sub_offsets = sorted(
        ((dx, dy) for dx in range(SIDE) for dy in range(SIDE)),
        key=lambda o: -ring(o[0], SIDE) - ring(o[1], SIDE),
    )
    subs = [((x + dx) % SIDE) * SIDE + (y + dy) % SIDE for dx, dy in sub_offsets]
    others = subs[:-1]
    sibling = (z * 2 + oc, sub)
    z_peers = [
        (((z + d) % DEPTH) * 2 + c, sub)
        for d in sorted(range(1, DEPTH), key=lambda d: -ring(d, DEPTH))
    ]

    loads = [
        pltpu.make_async_copy(
            pas_in.at[:, pl.ds(pl.multiple_of(c * HALF, HALF), HALF)],
            every.at[c, mine],
            load_sem.at[0],
        ),
        pltpu.make_async_copy(enc_in, enc, load_sem.at[1]),
        pltpu.make_async_copy(act_in, act, load_sem.at[2]),
        pltpu.make_async_copy(eb_in, eb, load_sem.at[3]),
        pltpu.make_async_copy(dec_in, dec, load_sem.at[4]),
        pltpu.make_async_copy(db_in, db, load_sem.at[5]),
    ]
    for load in loads:
        load.start()

    barrier = pltpu.get_barrier_semaphore()
    greeted = [(wide, s) for s in others] + [(zn * 2 + c, s) for s in others]
    greeted += z_peers + [sibling]
    for peer in greeted:
        pl.semaphore_signal(barrier, inc=1, device_id=peer, device_id_type=MESH)
    loads[0].wait()
    pl.semaphore_wait(barrier, len(greeted))

    pending = []

    def send(src, dst, k, peer):
        pltpu.make_async_remote_copy(
            src_ref=src, dst_ref=dst, send_sem=send_sem.at[k], recv_sem=recv_sem.at[k],
            device_id=peer, device_id_type=MESH,
        ).start()

    def arrived(ref, k):
        pltpu.make_async_copy(ref, ref, recv_sem.at[k]).wait()

    def sent(ref, k):
        pltpu.make_async_copy(ref, ref, send_sem.at[k]).wait()

    def swap(src, dst, k):
        copy = pltpu.make_async_remote_copy(
            src_ref=src, dst_ref=dst, send_sem=swap_send.at[k], recv_sem=swap_recv.at[k],
            device_id=sibling, device_id_type=MESH,
        )
        copy.start()
        pending.append(copy.wait_send)
        return copy

    def gather(array, k, swap_k):
        for s in others:
            send(array.at[c, mine], array.at[c, mine], k, (wide, s))
        rest = array.at[c, pl.ds(0, ROWS - OWN)]
        pending.append(lambda: sent(rest, k))
        arrived(rest, k)
        return swap(array.at[c], array.at[c], swap_k)

    def half(h):
        return pl.ds(pl.multiple_of(h * HALF, HALF), HALF)

    def quarter(q):
        return pl.ds(pl.multiple_of(q * QUARTER, QUARTER), QUARTER)

    def reduce_out(i, part):
        swaps = []
        for t in range(2):
            zq = zp if t else 1 - zp
            swap_out[i, t] = part(oc * 2 + zq).astype(BF16)
            swaps.append(swap(swap_out.at[i, t], swap_in.at[i, t], 2 + 2 * i + t))
        slot = zp * 16 + sub
        k = 2 + 2 * i
        for t in range(2):
            zq = zp if t else 1 - zp
            own = part(c * 2 + zq)
            swaps[t].wait_recv()
            parts[i, t] = (own + swap_in[i, t].astype(F32)).astype(BF16)
            for s in others if t else subs:
                rows = pl.ds(pl.multiple_of(s * OWN, OWN), OWN)
                peer = (wide if t else zn * 2 + c, s)
                send(parts.at[i, t, rows], rows_in.at[i, slot], k, peer)
        rows_in[i, slot] = parts[i, 1, mine]
        pending.append(lambda: sent(rows_in.at[i, pl.ds(0, 31)], k))

    def pieces_along_z(i):
        k = 2 + 2 * i
        arrived(rows_in.at[i, pl.ds(0, 31)], k)
        total = rows_in[i, 0].astype(F32)
        for n in range(1, 32):
            total = total + rows_in[i, n].astype(F32)
        rows_z[i, z] = total.astype(BF16)
        for peer in z_peers:
            send(rows_z.at[i, z], rows_z.at[i, z], k + 1, peer)
        pending.append(lambda: sent(rows_z.at[i, pl.ds(0, 15)], k + 1))

    def sum_along_z(i, zq):
        total = rows_z[i, zq].astype(F32)
        for n in range(1, DEPTH // 2):
            total = total + rows_z[i, 2 * n + zq].astype(F32)
        return total

    passages_swap = gather(every, 0, 0)
    loads[1].wait()
    pre[...] = dot_nn(every[c], enc[half(c), :])
    for load in loads[2:]:
        load.wait()
    passages_swap.wait_recv()
    both = pre[...] + dot_nn(every[oc], enc[half(oc), :]) + eb[...]
    codes[...] = (act[...].astype(F32) * both).astype(BF16)

    reduce_out(0, lambda q: dot_nn(codes[...], dec[:, quarter(q)]))
    codes_t[...] = codes[...].T
    pieces_along_z(0)
    every_t[0] = every[0].T
    every_t[1] = every[1].T
    arrived(rows_z.at[0, pl.ds(0, 15)], 3)
    for zq in range(2):
        recon = sum_along_z(0, zq) + db[:, quarter(c * 2 + zq)]
        columns = pl.ds(zq * QUARTER, QUARTER)
        resid[c, mine, columns] = (recon - every[c, mine, columns].astype(F32)).astype(BF16)
    resid_swap = gather(resid, 1, 1)
    pre[...] = dot_nt(resid[c], dec[:, half(c)])
    resid_swap.wait_recv()
    back = pre[...] + dot_nt(resid[oc], dec[:, half(oc)])
    dpre[...] = (act[...].astype(F32) * back).astype(BF16)

    reduce_out(1, lambda q: dot_nt(dpre[...], enc[quarter(q), :]))
    for h in range(2):
        gdec_out[:, pl.ds(h * HALF, HALF)] = dot_nn(codes_t[...], resid[h]).astype(BF16)
        gdb_out[:, pl.ds(h * HALF, HALF)] = jnp.sum(resid[h].astype(F32), axis=0, keepdims=True)
    for h in range(2):
        genc_out[pl.ds(h * HALF, HALF), :] = dot_nn(every_t[h], dpre[...]).astype(BF16)
    geb_out[...] = jnp.sum(dpre[...].astype(F32), axis=0, keepdims=True)
    pieces_along_z(1)
    arrived(rows_z.at[1, pl.ds(0, 15)], 5)
    for zq in range(2):
        final[c, :, pl.ds(zq * QUARTER, QUARTER)] = sum_along_z(1, zq)
    final_swap = swap(final.at[c], final.at[c], 6)
    final_swap.wait_recv()
    for wait in pending:
        wait()
    for h in range(2):
        gin_out[:, pl.ds(h * HALF, HALF)] = final[h] - resid[h, mine].astype(F32)


def place(genc_in, geb_in, gdec_in, gdb_in, gin_in, genc, geb, gdec, gdb, gin, sem):
    pairs = [(genc_in, genc), (gdec_in, gdec), (gin_in, gin), (geb_in, geb), (gdb_in, gdb)]
    copies = [pltpu.make_async_copy(a, b, sem.at[i]) for i, (a, b) in enumerate(pairs)]
    for copy in copies:
        copy.start()
    for copy in copies:
        copy.wait()


def per_device(passages, enc_weight, enc_bias, dec_weight, dec_bias, active):
    anywhere = pl.BlockSpec(memory_space=pl.ANY)
    vmem = pl.BlockSpec(memory_space=pltpu.VMEM)
    arrays = (
        passages, enc_weight, enc_bias.reshape(1, LAT), dec_weight, dec_bias.reshape(1, D), active
    )
    shapes = (
        jax.ShapeDtypeStruct((D, LAT), BF16),
        jax.ShapeDtypeStruct((1, LAT), F32),
        jax.ShapeDtypeStruct((LAT, D), BF16),
        jax.ShapeDtypeStruct((1, D), F32),
        jax.ShapeDtypeStruct((OWN, D), F32),
    )
    results = pl.pallas_call(
        kernel,
        out_shape=[pltpu.VMEM(s.shape, s.dtype) for s in shapes],
        in_specs=[pl.BlockSpec(memory_space=pltpu.HBM)] * 6,
        out_specs=[vmem] * 5,
        scratch_shapes=[
            pltpu.VMEM((D, LAT), BF16),
            pltpu.VMEM((LAT, D), BF16),
            pltpu.VMEM((ROWS, LAT), jnp.int32),
            pltpu.VMEM((1, LAT), F32),
            pltpu.VMEM((1, D), F32),
            pltpu.VMEM((2, ROWS, HALF), BF16),
            pltpu.VMEM((2, HALF, ROWS), BF16),
            pltpu.VMEM((ROWS, LAT), F32),
            pltpu.VMEM((ROWS, LAT), BF16),
            pltpu.VMEM((LAT, ROWS), BF16),
            pltpu.VMEM((2, ROWS, HALF), BF16),
            pltpu.VMEM((ROWS, LAT), BF16),
            pltpu.VMEM((2, 2, ROWS, QUARTER), BF16),
            pltpu.VMEM((2, 2, ROWS, QUARTER), BF16),
            pltpu.VMEM((2, 2, ROWS, QUARTER), BF16),
            pltpu.VMEM((2, 32, OWN, QUARTER), BF16),
            pltpu.VMEM((2, DEPTH, OWN, QUARTER), BF16),
            pltpu.VMEM((2, OWN, HALF), F32),
            pltpu.SemaphoreType.DMA((6,)),
            pltpu.SemaphoreType.DMA((6,)),
            pltpu.SemaphoreType.DMA((6,)),
            pltpu.SemaphoreType.DMA((7,)),
            pltpu.SemaphoreType.DMA((7,)),
        ],
        compiler_params=pltpu.CompilerParams(
            collective_id=0, has_side_effects=True, vmem_limit_bytes=40 * 2**20
        ),
        cost_estimate=pl.CostEstimate(
            flops=10 * ROWS * D * LAT, bytes_accessed=5 * 2**20, transcendentals=0
        ),
        name="sae_backward",
    )(*(pltpu.with_memory_space_constraint(a, pltpu.HBM) for a in arrays))
    genc, geb, gdec, gdb, gin = pl.pallas_call(
        place,
        out_shape=shapes,
        in_specs=[vmem] * 5,
        out_specs=[anywhere] * 5,
        scratch_shapes=[pltpu.SemaphoreType.DMA((5,))],
        compiler_params=pltpu.CompilerParams(vmem_limit_bytes=2**18),
        name="place",
    )(*(pltpu.with_memory_space_constraint(a, pltpu.VMEM) for a in results))
    return genc, geb.reshape(LAT), gdec, gdb.reshape(D), gin


def solution(mesh):
    split = P(None, ("wide", "sub"))
    rows = P(("wide", "sub"), None)
    line = P(("wide", "sub"))
    return jax.shard_map(
        per_device,
        mesh=mesh,
        in_specs=(P("sub", None), split, line, rows, P(), split),
        out_specs=(split, line, rows, P(), P("sub", None)),
        check_vma=False,
    )
```

```python
import jax
import jax.numpy as jnp
from jax import lax
from jax.experimental import pallas as pl
from jax.experimental.pallas import tpu as pltpu
from jax.sharding import PartitionSpec as P

MESH = pl.DeviceIdType.MESH
BF16 = jnp.bfloat16
F32 = jnp.float32
ROWS, D, LAT = 256, 1024, 512
OWN, HALF, QUARTER = 16, 512, 256
SIDE, DEPTH = 4, 16


def ring(d, n):
    return min(d, n - d)


OFFSETS = sorted(
    ((dx, dy) for dx in range(SIDE) for dy in range(SIDE)),
    key=lambda o: -ring(o[0], SIDE) - ring(o[1], SIDE),
)
BACK = [OFFSETS.index((-dx % SIDE, -dy % SIDE)) for dx, dy in OFFSETS]
PEERS = len(OFFSETS) - 1
FORWARD = ((11, 16), (8, 11), (5, 8), (3, 5), (1, 3), (0, 1))
CHUNKS = ((0, 5), (5, 11), (11, 16))
Z_STEPS = sorted(range(1, DEPTH), key=lambda d: -ring(d, DEPTH))


def blocks(first, last):
    return pl.ds(first * OWN, (last - first) * OWN)


def dot_nt(a, b):
    return lax.dot_general(a, b, (((1,), (1,)), ((), ())), preferred_element_type=F32)


def dot_nn(a, b):
    return jnp.dot(a, b, preferred_element_type=F32)


def kernel(
    pas_in, enc_in, eb_in, dec_in, db_in, act_in,
    genc_out, geb_out, gdec_out, gdb_out, gin_out,
    enc, dec, act, eb, db, every, every_t, pre, codes, codes_t, resid, dpre,
    swap_out, swap_in, parts, rows_in, rows_z, block_sums, final,
    load_sem, send_sem, block_sem, piece_sem, z_sem, swap_send, swap_recv, near_sem,
):
    wide, sub = lax.axis_index("wide"), lax.axis_index("sub")
    z, c = wide // 2, wide % 2
    x, y = sub // SIDE, sub % SIDE
    zp = z % 2
    oc = 1 - c
    mine = blocks(PEERS, PEERS + 1)

    def along_z(d):
        return (((z + d) % DEPTH) * 2 + c, sub)

    subs = [((x + dx) % SIDE) * SIDE + (y + dy) % SIDE for dx, dy in OFFSETS]
    other_plane = (z + 1 - 2 * zp) * 2 + c
    sibling = (z * 2 + oc, sub)

    def half(h):
        return pl.ds(pl.multiple_of(h * HALF, HALF), HALF)

    def quarter(q):
        return pl.ds(pl.multiple_of(q * QUARTER, QUARTER), QUARTER)

    own_load = pltpu.make_async_copy(pas_in.at[:, half(c)], every.at[c, mine], load_sem.at[0])
    enc_load = pltpu.make_async_copy(enc_in, enc, load_sem.at[1])
    loads = [
        pltpu.make_async_copy(eb_in, eb, load_sem.at[2]),
        pltpu.make_async_copy(dec_in, dec, load_sem.at[3]),
        pltpu.make_async_copy(db_in, db, load_sem.at[4]),
    ]

    barrier = pltpu.get_barrier_semaphore()
    own_load.start()
    greeted = [(wide, s) for s in subs[:PEERS]] + [sibling, along_z(1), along_z(DEPTH - 1)]
    for peer in greeted:
        pl.semaphore_signal(barrier, inc=1, device_id=peer, device_id_type=MESH)
    own_load.wait()
    pl.semaphore_wait(barrier, len(greeted))

    def tell(step):
        for d in (1 << step, DEPTH - (1 << step)):
            pl.semaphore_signal(
                near_sem.at[step], inc=1, device_id=along_z(d), device_id_type=MESH
            )

    def told(step):
        pl.semaphore_wait(near_sem.at[step], 2)

    pending = []

    def send(src, dst, k, recv, peer):
        pltpu.make_async_remote_copy(
            src_ref=src, dst_ref=dst, send_sem=send_sem.at[k], recv_sem=recv,
            device_id=peer, device_id_type=MESH,
        ).start()

    def wait(ref, sem):
        pltpu.make_async_copy(ref, ref, sem).wait()

    def forward(array, i, first, last):
        ref = array.at[c, ..., blocks(first, last), :]
        pltpu.make_async_remote_copy(
            src_ref=ref, dst_ref=ref, send_sem=swap_send.at[i], recv_sem=swap_recv.at[i],
            device_id=sibling, device_id_type=MESH,
        ).start()

    def forwarded(array, i):
        wait(array.at[oc], swap_recv.at[i])
        pending.append(lambda: wait(array.at[c], swap_send.at[i]))

    def reduce_out(i, part):
        swaps = []
        for n, (first, last) in enumerate(CHUNKS):
            rows = blocks(first, last)
            for t in range(2):
                q = oc * 2 + (zp if t else 1 - zp)
                swap_out[i, t, rows] = part(q, rows).astype(BF16)
            swap = pltpu.make_async_remote_copy(
                src_ref=swap_out.at[i, :, rows], dst_ref=swap_in.at[i, :, rows],
                send_sem=swap_send.at[2 + 3 * i + n], recv_sem=swap_recv.at[2 + 3 * i + n],
                device_id=sibling, device_id_type=MESH,
            )
            swap.start()
            swaps.append(swap)
        for swap, (first, last) in zip(swaps, CHUNKS):
            rows = blocks(first, last)
            own = [part(c * 2 + (zp if t else 1 - zp), rows) for t in range(2)]
            swap.wait_recv()
            for t in range(2):
                parts[i, t, rows] = (own[t] + swap_in[i, t, rows].astype(F32)).astype(BF16)
                for k in range(first, last):
                    if t and k == PEERS:
                        continue
                    send(
                        parts.at[i, t, blocks(k, k + 1)], rows_in.at[i, t, BACK[k]],
                        2 + 2 * i + t, piece_sem.at[i, t], (wide if t else other_plane, subs[k]),
                    )
            pending.append(swap.wait_send)
        rows_in[i, 1, PEERS] = parts[i, 1, mine]

        pending.append(lambda: wait(parts.at[i, 0], send_sem.at[2 + 2 * i]))
        pending.append(lambda: wait(parts.at[i, 1, blocks(0, PEERS)], send_sem.at[3 + 2 * i]))

    def pieces_in(i, slot):
        wait(rows_in.at[i, 1, pl.ds(0, PEERS)], piece_sem.at[i, 1])
        total = rows_in[i, 1, 0].astype(F32)
        for n in range(1, PEERS + 1):
            total = total + rows_in[i, 1, n].astype(F32)
        wait(rows_in.at[i, 0], piece_sem.at[i, 0])
        for n in range(PEERS + 1):
            total = total + rows_in[i, 0, n].astype(F32)
        rows_z[i, slot] = total.astype(BF16)

    for k in range(PEERS):
        there = every.at[c, blocks(BACK[k], BACK[k] + 1)]
        send(every.at[c, mine], there, 0, block_sem.at[0, BACK[k]], (wide, subs[k]))
    pending.append(lambda: wait(every.at[c, blocks(0, PEERS)], send_sem.at[0]))
    tell(0)
    enc_load.start()
    for k, s in enumerate(subs):
        rows = pl.ds(pl.multiple_of(s * OWN, OWN), OWN)
        pltpu.make_async_copy(act_in.at[rows], act.at[blocks(k, k + 1)], load_sem.at[5]).start()
    for load in loads:
        load.start()
    for n, (first, last) in enumerate(FORWARD):
        for k in range(min(last, PEERS) - 1, first - 1, -1):
            wait(every.at[c, blocks(k, k + 1)], block_sem.at[0, k])
        forward(every, 0, first, last)
        if n == 0:
            told(0)
            tell(1)
    enc_load.wait()
    for load in loads:
        load.wait()
    wait(act, load_sem.at[5])
    pre[...] = dot_nn(every[c], enc[half(c), :]) + eb[...]
    forwarded(every, 0)
    both = pre[...] + dot_nn(every[oc], enc[half(oc), :])
    codes[...] = (act[...].astype(F32) * both).astype(BF16)
    told(1)
    tell(2)

    reduce_out(0, lambda q, rows: dot_nn(codes[rows], dec[:, quarter(q)]))
    codes_t[...] = codes[...].T
    told(2)
    pieces_in(0, z // 2)
    for d in Z_STEPS:
        if d % 2 == 0:
            send(rows_z.at[0, z // 2], rows_z.at[0, z // 2], 6, z_sem.at[0], along_z(d))
    pending.append(lambda: wait(rows_z.at[0, pl.ds(0, DEPTH // 2 - 1)], send_sem.at[6]))
    every_t[0] = every[0].T
    every_t[1] = every[1].T
    wait(rows_z.at[0, pl.ds(0, DEPTH // 2 - 1)], z_sem.at[0])
    recon = rows_z[0, 0].astype(F32)
    for n in range(1, DEPTH // 2):
        recon = recon + rows_z[0, n].astype(F32)
    recon = recon + db[:, quarter(c * 2 + zp)]
    owned = every[c, mine, quarter(zp)].astype(F32)
    resid[c, zp, mine] = (recon - owned).astype(BF16)
    for k in range(PEERS + 1):
        for t in range(2):
            if t and k == PEERS:
                continue
            there = resid.at[c, zp, blocks(BACK[k], BACK[k] + 1)]
            recv = block_sem.at[1 + t, BACK[k]]
            send(resid.at[c, zp, mine], there, 8 if t else 1, recv, (wide if t else other_plane, subs[k]))
    pending.append(lambda: wait(rows_in.at[0, 0], send_sem.at[1]))
    pending.append(lambda: wait(rows_in.at[0, 1, pl.ds(0, PEERS)], send_sem.at[8]))
    for first, last in FORWARD:
        for k in range(last - 1, first - 1, -1):
            if k < PEERS:
                wait(resid.at[c, zp, blocks(k, k + 1)], block_sem.at[2, k])
            wait(resid.at[c, 1 - zp, blocks(k, k + 1)], block_sem.at[1, k])
        forward(resid, 1, first, last)
    back = dot_nt(resid[c, 0], dec[:, quarter(c * 2)])
    pre[...] = back + dot_nt(resid[c, 1], dec[:, quarter(c * 2 + 1)])
    forwarded(resid, 1)
    back = pre[...] + dot_nt(resid[oc, 0], dec[:, quarter(oc * 2)])
    back = back + dot_nt(resid[oc, 1], dec[:, quarter(oc * 2 + 1)])
    dpre[...] = (act[...].astype(F32) * back).astype(BF16)

    reduce_out(1, lambda q, rows: dot_nt(dpre[rows], enc[quarter(q), :]))
    for h in range(2):
        for n in range(2):
            gdec_out[:, quarter(2 * h + n)] = dot_nn(codes_t[...], resid[h, n]).astype(BF16)
        genc_out[half(h), :] = dot_nn(every_t[h], dpre[...]).astype(BF16)
    geb_out[...] = jnp.sum(dpre[...].astype(F32), axis=0, keepdims=True)
    pieces_in(1, z)
    for d in Z_STEPS:
        send(rows_z.at[1, z], rows_z.at[1, z], 7, z_sem.at[1], along_z(d))
    for q in range(4):
        for k, s in enumerate(subs):
            rows = resid[q // 2, q % 2, blocks(k, k + 1)].astype(F32)
            block_sums[pl.ds(s, 1), quarter(q)] = jnp.sum(rows, axis=0, keepdims=True)
    gdb_out[...] = jnp.sum(block_sums[...], axis=0, keepdims=True)
    for end in pending:
        end()
    pending.clear()
    everything = rows_z.at[1, pl.ds(0, DEPTH - 1)]
    wait(everything, z_sem.at[1])
    for zq in range(2):
        total = rows_z[1, zq].astype(F32)
        for n in range(1, DEPTH // 2):
            total = total + rows_z[1, 2 * n + zq].astype(F32)
        final[c, zq] = total
    final_swap = pltpu.make_async_remote_copy(
        src_ref=final.at[c], dst_ref=final.at[c],
        send_sem=swap_send.at[8], recv_sem=swap_recv.at[8],
        device_id=sibling, device_id_type=MESH,
    )
    final_swap.start()
    wait(everything, send_sem.at[7])
    for zq in range(2):
        gin_out[:, quarter(c * 2 + zq)] = final[c, zq] - resid[c, zq, mine].astype(F32)
    final_swap.wait()
    for zq in range(2):
        gin_out[:, quarter(oc * 2 + zq)] = final[oc, zq] - resid[oc, zq, mine].astype(F32)


def place(genc_in, geb_in, gdec_in, gdb_in, gin_in, genc, geb, gdec, gdb, gin, sem):
    pairs = [(gin_in, gin), (geb_in, geb), (gdb_in, gdb)]
    for whole_in, whole in ((genc_in, genc), (gdec_in, gdec)):
        step = whole.shape[0] // 4
        for n in range(4):
            rows = pl.ds(n * step, step)
            pairs.append((whole_in.at[rows], whole.at[rows]))
    copies = [pltpu.make_async_copy(a, b, sem.at[i]) for i, (a, b) in enumerate(pairs)]
    for copy in copies:
        copy.start()
    for copy in copies:
        copy.wait()


def per_device(passages, enc_weight, enc_bias, dec_weight, dec_bias, active):
    anywhere = pl.BlockSpec(memory_space=pl.ANY)
    vmem = pl.BlockSpec(memory_space=pltpu.VMEM)
    arrays = (
        passages, enc_weight, enc_bias.reshape(1, LAT), dec_weight, dec_bias.reshape(1, D), active
    )
    shapes = (
        jax.ShapeDtypeStruct((D, LAT), BF16),
        jax.ShapeDtypeStruct((1, LAT), F32),
        jax.ShapeDtypeStruct((LAT, D), BF16),
        jax.ShapeDtypeStruct((1, D), F32),
        jax.ShapeDtypeStruct((OWN, D), F32),
    )
    results = pl.pallas_call(
        kernel,
        out_shape=[pltpu.VMEM(s.shape, s.dtype) for s in shapes],
        in_specs=[pl.BlockSpec(memory_space=pltpu.HBM)] * 6,
        out_specs=[vmem] * 5,
        scratch_shapes=[
            pltpu.VMEM((D, LAT), BF16),
            pltpu.VMEM((LAT, D), BF16),
            pltpu.VMEM((ROWS, LAT), jnp.int32),
            pltpu.VMEM((1, LAT), F32),
            pltpu.VMEM((1, D), F32),
            pltpu.VMEM((2, ROWS, HALF), BF16),
            pltpu.VMEM((2, HALF, ROWS), BF16),
            pltpu.VMEM((ROWS, LAT), F32),
            pltpu.VMEM((ROWS, LAT), BF16),
            pltpu.VMEM((LAT, ROWS), BF16),
            pltpu.VMEM((2, 2, ROWS, QUARTER), BF16),
            pltpu.VMEM((ROWS, LAT), BF16),
            pltpu.VMEM((2, 2, ROWS, QUARTER), BF16),
            pltpu.VMEM((2, 2, ROWS, QUARTER), BF16),
            pltpu.VMEM((2, 2, ROWS, QUARTER), BF16),
            pltpu.VMEM((2, 2, PEERS + 1, OWN, QUARTER), BF16),
            pltpu.VMEM((2, DEPTH, OWN, QUARTER), BF16),
            pltpu.VMEM((PEERS + 1, D), F32),
            pltpu.VMEM((2, 2, OWN, QUARTER), F32),
            pltpu.SemaphoreType.DMA((6,)),
            pltpu.SemaphoreType.DMA((9,)),
            pltpu.SemaphoreType.DMA((3, PEERS + 1)),
            pltpu.SemaphoreType.DMA((2, 2)),
            pltpu.SemaphoreType.DMA((2,)),
            pltpu.SemaphoreType.DMA((9,)),
            pltpu.SemaphoreType.DMA((9,)),
            pltpu.SemaphoreType.REGULAR((3,)),
        ],
        compiler_params=pltpu.CompilerParams(
            collective_id=0, has_side_effects=True, vmem_limit_bytes=40 * 2**20
        ),
        cost_estimate=pl.CostEstimate(
            flops=10 * ROWS * D * LAT, bytes_accessed=5 * 2**20, transcendentals=0
        ),
        name="sae_backward",
    )(*(pltpu.with_memory_space_constraint(a, pltpu.HBM) for a in arrays))
    genc, geb, gdec, gdb, gin = pl.pallas_call(
        place,
        out_shape=shapes,
        in_specs=[vmem] * 5,
        out_specs=[anywhere] * 5,
        scratch_shapes=[pltpu.SemaphoreType.DMA((11,))],
        compiler_params=pltpu.CompilerParams(vmem_limit_bytes=2**18),
        name="place",
    )(*(pltpu.with_memory_space_constraint(a, pltpu.VMEM) for a in results))
    return genc, geb.reshape(LAT), gdec, gdb.reshape(D), gin


def solution(mesh):
    split = P(None, ("wide", "sub"))
    rows = P(("wide", "sub"), None)
    line = P(("wide", "sub"))
    return jax.shard_map(
        per_device,
        mesh=mesh,
        in_specs=(P("sub", None), split, line, rows, P(), split),
        out_specs=(split, line, rows, P(), P("sub", None)),
        check_vma=False,
    )
```

```python
import jax
import jax.numpy as jnp
from jax import lax
from jax.experimental import pallas as pl
from jax.experimental.pallas import tpu as pltpu
from jax.sharding import PartitionSpec as P

MESH = pl.DeviceIdType.MESH
BF16 = jnp.bfloat16
F32 = jnp.float32
ROWS, D, LAT = 256, 1024, 512
OWN, HALF, QUARTER = 16, 512, 256
SIDE, DEPTH = 4, 16


def ring(d, n):
    return min(d, n - d)


OFFSETS = sorted(
    ((dx, dy) for dx in range(SIDE) for dy in range(SIDE)),
    key=lambda o: -ring(o[0], SIDE) - ring(o[1], SIDE),
)
BACK = [OFFSETS.index((-dx % SIDE, -dy % SIDE)) for dx, dy in OFFSETS]
PEERS = len(OFFSETS) - 1
FORWARD = ((11, 16), (8, 11), (5, 8), (3, 5), (1, 3), (0, 1))
CHUNKS = ((0, 5), (5, 11), (11, 16))
Z_STEPS = sorted(range(1, DEPTH), key=lambda d: -ring(d, DEPTH))


def blocks(first, last):
    return pl.ds(first * OWN, (last - first) * OWN)


def dot_nn(a, b):
    return jnp.dot(a, b, preferred_element_type=F32)


def kernel(
    pas_in, enc_in, eb_in, dec_in, db_in, act_in,
    genc_out, geb_out, gdec_out, gdb_out, gin_out,
    enc, enc_t, dec, dec_t, act, eb, db, every, every_t, pre, own, codes, codes_t, resid, dpre,
    swap_out, swap_in, parts, rows_in, rows_z, block_sums, final,
    load_sem, send_sem, block_sem, piece_sem, z_sem, swap_send, swap_recv, mate_sem, near_sem,
):
    wide, sub = lax.axis_index("wide"), lax.axis_index("sub")
    z, c = wide // 2, wide % 2
    x, y = sub // SIDE, sub % SIDE
    zp = z % 2
    oc = 1 - c
    mine = blocks(PEERS, PEERS + 1)

    def along_z(d):
        return (((z + d) % DEPTH) * 2 + c, sub)

    subs = [((x + dx) % SIDE) * SIDE + (y + dy) % SIDE for dx, dy in OFFSETS]
    other_plane = (z + 1 - 2 * zp) * 2 + c
    sibling = (z * 2 + oc, sub)

    def half(h):
        return pl.ds(pl.multiple_of(h * HALF, HALF), HALF)

    def quarter(q):
        return pl.ds(pl.multiple_of(q * QUARTER, QUARTER), QUARTER)

    own_load = pltpu.make_async_copy(pas_in.at[:, half(c)], every.at[c, mine], load_sem.at[0])
    enc_load = pltpu.make_async_copy(enc_in, enc, load_sem.at[1])
    loads = [
        pltpu.make_async_copy(eb_in, eb, load_sem.at[2]),
        pltpu.make_async_copy(dec_in, dec, load_sem.at[3]),
        pltpu.make_async_copy(db_in, db, load_sem.at[4]),
    ]

    barrier = pltpu.get_barrier_semaphore()
    own_load.start()
    greeted = [(wide, s) for s in subs[:PEERS]] + [sibling, along_z(1), along_z(DEPTH - 1)]
    for peer in greeted:
        pl.semaphore_signal(barrier, inc=1, device_id=peer, device_id_type=MESH)
    own_load.wait()
    pl.semaphore_wait(barrier, len(greeted))

    def tell(step):
        for d in (1 << step, DEPTH - (1 << step)):
            pl.semaphore_signal(
                near_sem.at[step], inc=1, device_id=along_z(d), device_id_type=MESH
            )

    def told(step):
        pl.semaphore_wait(near_sem.at[step], 2)

    pending = []

    def send(src, dst, k, recv, peer):
        pltpu.make_async_remote_copy(
            src_ref=src, dst_ref=dst, send_sem=send_sem.at[k], recv_sem=recv,
            device_id=peer, device_id_type=MESH,
        ).start()

    def wait(ref, sem):
        pltpu.make_async_copy(ref, ref, sem).wait()

    def forward(array, i, first, last):
        ref = array.at[c, ..., blocks(first, last), :]
        pltpu.make_async_remote_copy(
            src_ref=ref, dst_ref=ref, send_sem=swap_send.at[i], recv_sem=swap_recv.at[i],
            device_id=sibling, device_id_type=MESH,
        ).start()

    def forwarded(array, i):
        wait(array.at[oc], swap_recv.at[i])
        pending.append(lambda: wait(array.at[c], swap_send.at[i]))

    def reduce_out(i, part):
        swaps = []
        planes = (1 - zp, zp)
        for t in range(2):
            swap_out[i, t] = part(oc * 2 + planes[t]).astype(BF16)
        for n, (first, last) in enumerate(CHUNKS):
            rows = blocks(first, last)
            swap = pltpu.make_async_remote_copy(
                src_ref=swap_out.at[i, :, rows], dst_ref=swap_in.at[i, :, rows],
                send_sem=swap_send.at[2 + 3 * i + n], recv_sem=swap_recv.at[2 + 3 * i + n],
                device_id=sibling, device_id_type=MESH,
            )
            swap.start()
            swaps.append(swap)
        for t in range(2):
            own[t] = part(c * 2 + planes[t])
        for swap, (first, last) in zip(swaps, CHUNKS):
            rows = blocks(first, last)
            swap.wait_recv()
            for t in range(2):
                parts[i, t, rows] = (own[t, rows] + swap_in[i, t, rows].astype(F32)).astype(BF16)
                for k in range(first, last):
                    if t and k == PEERS:
                        continue
                    send(
                        parts.at[i, t, blocks(k, k + 1)], rows_in.at[i, t, BACK[k]],
                        2 + 2 * i + t, piece_sem.at[i, t], (wide if t else other_plane, subs[k]),
                    )
            pending.append(swap.wait_send)
        rows_in[i, 1, PEERS] = parts[i, 1, mine]

        pending.append(lambda: wait(parts.at[i, 0], send_sem.at[2 + 2 * i]))
        pending.append(lambda: wait(parts.at[i, 1, blocks(0, PEERS)], send_sem.at[3 + 2 * i]))

    def pieces_in(i, slot):
        wait(rows_in.at[i, 1, pl.ds(0, PEERS)], piece_sem.at[i, 1])
        total = rows_in[i, 1, 0].astype(F32)
        for n in range(1, PEERS + 1):
            total = total + rows_in[i, 1, n].astype(F32)
        wait(rows_in.at[i, 0], piece_sem.at[i, 0])
        for n in range(PEERS + 1):
            total = total + rows_in[i, 0, n].astype(F32)
        rows_z[i, slot] = total.astype(BF16)

    def send_z(i):
        piece = rows_z.at[i, z // 2]
        for d in Z_STEPS:
            if d % 2 == 0:
                send(piece, piece, 6 + i, z_sem.at[i], along_z(d))
        pending.append(lambda: wait(z_others(i), send_sem.at[6 + i]))

    def z_others(i):
        return rows_z.at[i, pl.ds(0, DEPTH // 2 - 1)]

    def sum_along_z(i):
        wait(z_others(i), z_sem.at[i])
        total = rows_z[i, 0].astype(F32)
        for n in range(1, DEPTH // 2):
            total = total + rows_z[i, n].astype(F32)
        return total

    for k in range(PEERS):
        there = every.at[c, blocks(BACK[k], BACK[k] + 1)]
        send(every.at[c, mine], there, 0, block_sem.at[0, BACK[k]], (wide, subs[k]))
    pending.append(lambda: wait(every.at[c, blocks(0, PEERS)], send_sem.at[0]))
    tell(0)
    enc_load.start()
    for k, s in enumerate(subs):
        rows = pl.ds(pl.multiple_of(s * OWN, OWN), OWN)
        pltpu.make_async_copy(act_in.at[rows], act.at[blocks(k, k + 1)], load_sem.at[5]).start()
    for load in loads:
        load.start()
    for n, (first, last) in enumerate(FORWARD):
        for k in range(min(last, PEERS) - 1, first - 1, -1):
            wait(every.at[c, blocks(k, k + 1)], block_sem.at[0, k])
        forward(every, 0, first, last)
    enc_load.wait()
    for load in loads:
        load.wait()
    wait(act, load_sem.at[5])
    pre[...] = dot_nn(every[c], enc[half(c), :]) + eb[...]
    told(0)
    tell(1)
    forwarded(every, 0)
    both = pre[...] + dot_nn(every[oc], enc[half(oc), :])
    codes[...] = (act[...].astype(F32) * both).astype(BF16)

    reduce_out(0, lambda q: dot_nn(codes[...], dec[:, quarter(q)]))
    told(1)
    tell(2)
    codes_t[...] = codes[...].T
    every_t[0] = every[0].T
    every_t[1] = every[1].T
    told(2)
    pieces_in(0, z // 2)
    send_z(0)
    dec_t[...] = dec[...].T
    enc_t[...] = enc[...].T
    recon = sum_along_z(0)
    recon = recon + db[:, quarter(c * 2 + zp)]
    owned = every[c, mine, quarter(zp)].astype(F32)
    resid[c, zp, mine] = (recon - owned).astype(BF16)
    for k in range(PEERS + 1):
        for t in range(2):
            if t and k == PEERS:
                continue
            there = resid.at[c, zp, blocks(BACK[k], BACK[k] + 1)]
            recv = block_sem.at[1 + t, BACK[k]]
            send(resid.at[c, zp, mine], there, 8 if t else 1, recv, (wide if t else other_plane, subs[k]))
    pending.append(lambda: wait(rows_in.at[0, 0], send_sem.at[1]))
    pending.append(lambda: wait(rows_in.at[0, 1, pl.ds(0, PEERS)], send_sem.at[8]))
    for first, last in FORWARD:
        for k in range(last - 1, first - 1, -1):
            if k < PEERS:
                wait(resid.at[c, zp, blocks(k, k + 1)], block_sem.at[2, k])
            wait(resid.at[c, 1 - zp, blocks(k, k + 1)], block_sem.at[1, k])
        forward(resid, 1, first, last)
    back = dot_nn(resid[c, 0], dec_t[quarter(c * 2), :])
    pre[...] = back + dot_nn(resid[c, 1], dec_t[quarter(c * 2 + 1), :])
    forwarded(resid, 1)
    back = pre[...] + dot_nn(resid[oc, 0], dec_t[quarter(oc * 2), :])
    back = back + dot_nn(resid[oc, 1], dec_t[quarter(oc * 2 + 1), :])
    dpre[...] = (act[...].astype(F32) * back).astype(BF16)

    reduce_out(1, lambda q: dot_nn(dpre[...], enc_t[:, quarter(q)]))
    for h in range(2):
        for n in range(2):
            gdec_out[:, quarter(2 * h + n)] = dot_nn(codes_t[...], resid[h, n]).astype(BF16)
        genc_out[half(h), :] = dot_nn(every_t[h], dpre[...]).astype(BF16)
    geb_out[...] = jnp.sum(dpre[...].astype(F32), axis=0, keepdims=True)
    pieces_in(1, z // 2)
    send_z(1)
    for q in range(4):
        for k, s in enumerate(subs):
            rows = resid[q // 2, q % 2, blocks(k, k + 1)].astype(F32)
            block_sums[pl.ds(s, 1), quarter(q)] = jnp.sum(rows, axis=0, keepdims=True)
    gdb_out[...] = jnp.sum(block_sums[...], axis=0, keepdims=True)
    for end in pending:
        end()
    pending.clear()
    q = c * 2 + zp
    final[q] = sum_along_z(1)
    mates = [(other_plane, sub), (other_plane + oc - c, sub), sibling]
    for n, peer in enumerate(mates):
        pltpu.make_async_remote_copy(
            src_ref=final.at[q], dst_ref=final.at[q],
            send_sem=mate_sem.at[0, n], recv_sem=mate_sem.at[1, n],
            device_id=peer, device_id_type=MESH,
        ).start()
    gin_out[:, quarter(q)] = final[q] - resid[c, zp, mine].astype(F32)
    for n, (h, zq) in ((2, (oc, zp)), (0, (c, 1 - zp)), (1, (oc, 1 - zp))):
        q = h * 2 + zq
        wait(final.at[q], mate_sem.at[1, n])
        gin_out[:, quarter(q)] = final[q] - resid[h, zq, mine].astype(F32)
    for n in range(3):
        wait(final.at[0], mate_sem.at[0, n])


def place(genc_in, geb_in, gdec_in, gdb_in, gin_in, genc, geb, gdec, gdb, gin, sem):
    pairs = [(genc_in, genc), (gdec_in, gdec), (gin_in, gin), (geb_in, geb), (gdb_in, gdb)]
    copies = [pltpu.make_async_copy(a, b, sem.at[i]) for i, (a, b) in enumerate(pairs)]
    for copy in copies:
        copy.start()
    for copy in copies:
        copy.wait()


def per_device(passages, enc_weight, enc_bias, dec_weight, dec_bias, active):
    anywhere = pl.BlockSpec(memory_space=pl.ANY)
    vmem = pl.BlockSpec(memory_space=pltpu.VMEM)
    arrays = (
        passages, enc_weight, enc_bias.reshape(1, LAT), dec_weight, dec_bias.reshape(1, D), active
    )
    shapes = (
        jax.ShapeDtypeStruct((D, LAT), BF16),
        jax.ShapeDtypeStruct((1, LAT), F32),
        jax.ShapeDtypeStruct((LAT, D), BF16),
        jax.ShapeDtypeStruct((1, D), F32),
        jax.ShapeDtypeStruct((OWN, D), F32),
    )
    results = pl.pallas_call(
        kernel,
        out_shape=[pltpu.VMEM(s.shape, s.dtype) for s in shapes],
        in_specs=[pl.BlockSpec(memory_space=pltpu.HBM)] * 6,
        out_specs=[vmem] * 5,
        scratch_shapes=[
            pltpu.VMEM((D, LAT), BF16),
            pltpu.VMEM((LAT, D), BF16),
            pltpu.VMEM((LAT, D), BF16),
            pltpu.VMEM((D, LAT), BF16),
            pltpu.VMEM((ROWS, LAT), jnp.int32),
            pltpu.VMEM((1, LAT), F32),
            pltpu.VMEM((1, D), F32),
            pltpu.VMEM((2, ROWS, HALF), BF16),
            pltpu.VMEM((2, HALF, ROWS), BF16),
            pltpu.VMEM((ROWS, LAT), F32),
            pltpu.VMEM((2, ROWS, QUARTER), F32),
            pltpu.VMEM((ROWS, LAT), BF16),
            pltpu.VMEM((LAT, ROWS), BF16),
            pltpu.VMEM((2, 2, ROWS, QUARTER), BF16),
            pltpu.VMEM((ROWS, LAT), BF16),
            pltpu.VMEM((2, 2, ROWS, QUARTER), BF16),
            pltpu.VMEM((2, 2, ROWS, QUARTER), BF16),
            pltpu.VMEM((2, 2, ROWS, QUARTER), BF16),
            pltpu.VMEM((2, 2, PEERS + 1, OWN, QUARTER), BF16),
            pltpu.VMEM((2, DEPTH // 2, OWN, QUARTER), BF16),
            pltpu.VMEM((PEERS + 1, D), F32),
            pltpu.VMEM((4, OWN, QUARTER), F32),
            pltpu.SemaphoreType.DMA((6,)),
            pltpu.SemaphoreType.DMA((9,)),
            pltpu.SemaphoreType.DMA((3, PEERS + 1)),
            pltpu.SemaphoreType.DMA((2, 2)),
            pltpu.SemaphoreType.DMA((2,)),
            pltpu.SemaphoreType.DMA((9,)),
            pltpu.SemaphoreType.DMA((9,)),
            pltpu.SemaphoreType.DMA((2, 3)),
            pltpu.SemaphoreType.REGULAR((3,)),
        ],
        compiler_params=pltpu.CompilerParams(
            collective_id=0, has_side_effects=True, vmem_limit_bytes=40 * 2**20
        ),
        cost_estimate=pl.CostEstimate(
            flops=10 * ROWS * D * LAT, bytes_accessed=5 * 2**20, transcendentals=0
        ),
        name="sae_backward",
    )(*(pltpu.with_memory_space_constraint(a, pltpu.HBM) for a in arrays))
    genc, geb, gdec, gdb, gin = pl.pallas_call(
        place,
        out_shape=shapes,
        in_specs=[vmem] * 5,
        out_specs=[anywhere] * 5,
        scratch_shapes=[pltpu.SemaphoreType.DMA((5,))],
        compiler_params=pltpu.CompilerParams(vmem_limit_bytes=2**18),
        name="place",
    )(*(pltpu.with_memory_space_constraint(a, pltpu.VMEM) for a in results))
    return genc, geb.reshape(LAT), gdec, gdb.reshape(D), gin


def solution(mesh):
    split = P(None, ("wide", "sub"))
    rows = P(("wide", "sub"), None)
    line = P(("wide", "sub"))
    return jax.shard_map(
        per_device,
        mesh=mesh,
        in_specs=(P("sub", None), split, line, rows, P(), split),
        out_specs=(split, line, rows, P(), P("sub", None)),
        check_vma=False,
    )
```

```python
import jax
import jax.numpy as jnp
from jax import lax
from jax.experimental import pallas as pl
from jax.experimental.pallas import tpu as pltpu
from jax.sharding import PartitionSpec as P

MESH = pl.DeviceIdType.MESH
BF16 = jnp.bfloat16
F32 = jnp.float32
ROWS, D, LAT = 256, 1024, 512
OWN, HALF, QUARTER = 16, 512, 256
SIDE, DEPTH = 4, 16


def ring(d, n):
    return min(d, n - d)


OFFSETS = sorted(
    ((dx, dy) for dx in range(SIDE) for dy in range(SIDE)),
    key=lambda o: -ring(o[0], SIDE) - ring(o[1], SIDE),
)
BACK = [OFFSETS.index((-dx % SIDE, -dy % SIDE)) for dx, dy in OFFSETS]
PEERS = len(OFFSETS) - 1
FORWARD = ((11, 16), (8, 11), (5, 8), (3, 5), (1, 3), (0, 1))
Z_STEPS = sorted(range(1, DEPTH), key=lambda d: -ring(d, DEPTH))


def blocks(first, last):
    return pl.ds(first * OWN, (last - first) * OWN)


def dot_nn(a, b):
    return jnp.dot(a, b, preferred_element_type=F32)


def kernel(
    pas_in, enc_in, eb_in, dec_in, db_in, act_in,
    genc_out, geb_out, gdec_out, gdb_out, gin_out,
    enc, enc_t, dec, dec_t, act, eb, db, every, every_t, pre, own, codes, codes_t, resid, dpre,
    swap_out, swap_in, parts, rows_in, rows_z, block_sums, final,
    load_sem, send_sem, block_sem, piece_sem, z_sem, swap_send, swap_recv, mate_sem, near_sem,
):
    wide, sub = lax.axis_index("wide"), lax.axis_index("sub")
    z, c = wide // 2, wide % 2
    x, y = sub // SIDE, sub % SIDE
    zp = z % 2
    oc = 1 - c
    mine = blocks(PEERS, PEERS + 1)

    def along_z(d):
        return (((z + d) % DEPTH) * 2 + c, sub)

    subs = [((x + dx) % SIDE) * SIDE + (y + dy) % SIDE for dx, dy in OFFSETS]
    other_plane = (z + 1 - 2 * zp) * 2 + c
    sibling = (z * 2 + oc, sub)

    def half(h):
        return pl.ds(pl.multiple_of(h * HALF, HALF), HALF)

    def quarter(q):
        return pl.ds(pl.multiple_of(q * QUARTER, QUARTER), QUARTER)

    own_load = pltpu.make_async_copy(pas_in.at[:, half(c)], every.at[c, mine], load_sem.at[0])
    enc_load = pltpu.make_async_copy(enc_in, enc, load_sem.at[1])
    loads = [
        pltpu.make_async_copy(eb_in, eb, load_sem.at[2]),
        pltpu.make_async_copy(dec_in, dec, load_sem.at[3]),
        pltpu.make_async_copy(db_in, db, load_sem.at[4]),
    ]

    barrier = pltpu.get_barrier_semaphore()
    own_load.start()
    greeted = [(wide, s) for s in subs[:PEERS]] + [sibling, along_z(1), along_z(DEPTH - 1)]
    for peer in greeted:
        pl.semaphore_signal(barrier, inc=1, device_id=peer, device_id_type=MESH)
    own_load.wait()
    pl.semaphore_wait(barrier, len(greeted))

    def tell(step):
        for d in (1 << step, DEPTH - (1 << step)):
            pl.semaphore_signal(
                near_sem.at[step], inc=1, device_id=along_z(d), device_id_type=MESH
            )

    def told(step):
        pl.semaphore_wait(near_sem.at[step], 2)

    pending = []

    def send(src, dst, k, recv, peer):
        pltpu.make_async_remote_copy(
            src_ref=src, dst_ref=dst, send_sem=send_sem.at[k], recv_sem=recv,
            device_id=peer, device_id_type=MESH,
        ).start()

    def wait(ref, sem):
        pltpu.make_async_copy(ref, ref, sem).wait()

    def forward(array, i, first, last):
        ref = array.at[c, ..., blocks(first, last), :]
        pltpu.make_async_remote_copy(
            src_ref=ref, dst_ref=ref, send_sem=swap_send.at[i], recv_sem=swap_recv.at[i],
            device_id=sibling, device_id_type=MESH,
        ).start()

    def forwarded(array, i):
        wait(array.at[oc], swap_recv.at[i])
        pending.append(lambda: wait(array.at[c], swap_send.at[i]))

    def reduce_out(i, part):
        swaps = []
        planes = (1 - zp, zp)
        for t in range(2):
            swap_out[i, t] = part(oc * 2 + planes[t]).astype(BF16)
            swap = pltpu.make_async_remote_copy(
                src_ref=swap_out.at[i, t], dst_ref=swap_in.at[i, t],
                send_sem=swap_send.at[2 + 3 * i + t], recv_sem=swap_recv.at[2 + 3 * i + t],
                device_id=sibling, device_id_type=MESH,
            )
            swap.start()
            swaps.append(swap)
        for t in range(2):
            own[t] = part(c * 2 + planes[t])
        for t, swap in enumerate(swaps):
            swap.wait_recv()
            parts[i, t] = (own[t] + swap_in[i, t].astype(F32)).astype(BF16)
            for k in range(PEERS + 1):
                if t and k == PEERS:
                    continue
                send(
                    parts.at[i, t, blocks(k, k + 1)], rows_in.at[i, t, BACK[k]],
                    2 + 2 * i + t, piece_sem.at[i, t], (wide if t else other_plane, subs[k]),
                )
            pending.append(swap.wait_send)
        rows_in[i, 1, PEERS] = parts[i, 1, mine]

        pending.append(lambda: wait(parts.at[i, 0], send_sem.at[2 + 2 * i]))
        pending.append(lambda: wait(parts.at[i, 1, blocks(0, PEERS)], send_sem.at[3 + 2 * i]))

    def pieces_in(i, slot):
        wait(rows_in.at[i, 1, pl.ds(0, PEERS)], piece_sem.at[i, 1])
        total = rows_in[i, 1, 0].astype(F32)
        for n in range(1, PEERS + 1):
            total = total + rows_in[i, 1, n].astype(F32)
        wait(rows_in.at[i, 0], piece_sem.at[i, 0])
        for n in range(PEERS + 1):
            total = total + rows_in[i, 0, n].astype(F32)
        rows_z[i, slot] = total.astype(BF16)

    def send_z(i):
        piece = rows_z.at[i, z // 2]
        for d in Z_STEPS:
            if d % 2 == 0:
                send(piece, piece, 6 + i, z_sem.at[i], along_z(d))
        pending.append(lambda: wait(z_others(i), send_sem.at[6 + i]))

    def z_others(i):
        return rows_z.at[i, pl.ds(0, DEPTH // 2 - 1)]

    def sum_along_z(i):
        wait(z_others(i), z_sem.at[i])
        total = rows_z[i, 0].astype(F32)
        for n in range(1, DEPTH // 2):
            total = total + rows_z[i, n].astype(F32)
        return total

    for k in range(PEERS):
        there = every.at[c, blocks(BACK[k], BACK[k] + 1)]
        send(every.at[c, mine], there, 0, block_sem.at[0, BACK[k]], (wide, subs[k]))
    pending.append(lambda: wait(every.at[c, blocks(0, PEERS)], send_sem.at[0]))
    tell(0)
    enc_load.start()
    for k, s in enumerate(subs):
        rows = pl.ds(pl.multiple_of(s * OWN, OWN), OWN)
        pltpu.make_async_copy(act_in.at[rows], act.at[blocks(k, k + 1)], load_sem.at[5]).start()
    for load in loads:
        load.start()
    for n, (first, last) in enumerate(FORWARD):
        for k in range(min(last, PEERS) - 1, first - 1, -1):
            wait(every.at[c, blocks(k, k + 1)], block_sem.at[0, k])
        forward(every, 0, first, last)
    enc_load.wait()
    for load in loads:
        load.wait()
    wait(act, load_sem.at[5])
    pre[...] = dot_nn(every[c], enc[half(c), :]) + eb[...]
    told(0)
    tell(1)
    forwarded(every, 0)
    both = pre[...] + dot_nn(every[oc], enc[half(oc), :])
    codes[...] = (act[...].astype(F32) * both).astype(BF16)

    reduce_out(0, lambda q: dot_nn(codes[...], dec[:, quarter(q)]))
    told(1)
    tell(2)
    codes_t[...] = codes[...].T
    every_t[0] = every[0].T
    every_t[1] = every[1].T
    told(2)
    pieces_in(0, z // 2)
    send_z(0)
    dec_t[...] = dec[...].T
    enc_t[...] = enc[...].T
    recon = sum_along_z(0)
    recon = recon + db[:, quarter(c * 2 + zp)]
    owned = every[c, mine, quarter(zp)].astype(F32)
    resid[c, zp, mine] = (recon - owned).astype(BF16)
    for k in range(PEERS + 1):
        for t in range(2):
            if t and k == PEERS:
                continue
            there = resid.at[c, zp, blocks(BACK[k], BACK[k] + 1)]
            recv = block_sem.at[1 + t, BACK[k]]
            send(resid.at[c, zp, mine], there, 8 if t else 1, recv, (wide if t else other_plane, subs[k]))
    pending.append(lambda: wait(rows_in.at[0, 0], send_sem.at[1]))
    pending.append(lambda: wait(rows_in.at[0, 1, pl.ds(0, PEERS)], send_sem.at[8]))
    for first, last in FORWARD:
        for k in range(last - 1, first - 1, -1):
            if k < PEERS:
                wait(resid.at[c, zp, blocks(k, k + 1)], block_sem.at[2, k])
            wait(resid.at[c, 1 - zp, blocks(k, k + 1)], block_sem.at[1, k])
        forward(resid, 1, first, last)
    back = dot_nn(resid[c, 0], dec_t[quarter(c * 2), :])
    pre[...] = back + dot_nn(resid[c, 1], dec_t[quarter(c * 2 + 1), :])
    forwarded(resid, 1)
    back = pre[...] + dot_nn(resid[oc, 0], dec_t[quarter(oc * 2), :])
    back = back + dot_nn(resid[oc, 1], dec_t[quarter(oc * 2 + 1), :])
    dpre[...] = (act[...].astype(F32) * back).astype(BF16)

    reduce_out(1, lambda q: dot_nn(dpre[...], enc_t[:, quarter(q)]))
    for h in range(2):
        for n in range(2):
            gdec_out[:, quarter(2 * h + n)] = dot_nn(codes_t[...], resid[h, n]).astype(BF16)
        genc_out[half(h), :] = dot_nn(every_t[h], dpre[...]).astype(BF16)
    geb_out[...] = jnp.sum(dpre[...].astype(F32), axis=0, keepdims=True)
    pieces_in(1, z // 2)
    send_z(1)
    for q in range(4):
        for k, s in enumerate(subs):
            rows = resid[q // 2, q % 2, blocks(k, k + 1)].astype(F32)
            block_sums[pl.ds(s, 1), quarter(q)] = jnp.sum(rows, axis=0, keepdims=True)
    gdb_out[...] = jnp.sum(block_sums[...], axis=0, keepdims=True)
    for end in pending:
        end()
    pending.clear()
    q = c * 2 + zp
    final[q] = sum_along_z(1)
    mates = [(other_plane, sub), (other_plane + oc - c, sub), sibling]
    for n, peer in enumerate(mates):
        pltpu.make_async_remote_copy(
            src_ref=final.at[q], dst_ref=final.at[q],
            send_sem=mate_sem.at[0, n], recv_sem=mate_sem.at[1, n],
            device_id=peer, device_id_type=MESH,
        ).start()
    gin_out[:, quarter(q)] = final[q] - resid[c, zp, mine].astype(F32)
    for n, (h, zq) in ((2, (oc, zp)), (0, (c, 1 - zp)), (1, (oc, 1 - zp))):
        q = h * 2 + zq
        wait(final.at[q], mate_sem.at[1, n])
        gin_out[:, quarter(q)] = final[q] - resid[h, zq, mine].astype(F32)
    for n in range(3):
        wait(final.at[0], mate_sem.at[0, n])


def place(genc_in, geb_in, gdec_in, gdb_in, gin_in, genc, geb, gdec, gdb, gin, sem):
    pairs = [(genc_in, genc), (gdec_in, gdec), (gin_in, gin), (geb_in, geb), (gdb_in, gdb)]
    copies = [pltpu.make_async_copy(a, b, sem.at[i]) for i, (a, b) in enumerate(pairs)]
    for copy in copies:
        copy.start()
    for copy in copies:
        copy.wait()


def per_device(passages, enc_weight, enc_bias, dec_weight, dec_bias, active):
    anywhere = pl.BlockSpec(memory_space=pl.ANY)
    vmem = pl.BlockSpec(memory_space=pltpu.VMEM)
    arrays = (
        passages, enc_weight, enc_bias.reshape(1, LAT), dec_weight, dec_bias.reshape(1, D), active
    )
    shapes = (
        jax.ShapeDtypeStruct((D, LAT), BF16),
        jax.ShapeDtypeStruct((1, LAT), F32),
        jax.ShapeDtypeStruct((LAT, D), BF16),
        jax.ShapeDtypeStruct((1, D), F32),
        jax.ShapeDtypeStruct((OWN, D), F32),
    )
    results = pl.pallas_call(
        kernel,
        out_shape=[pltpu.VMEM(s.shape, s.dtype) for s in shapes],
        in_specs=[pl.BlockSpec(memory_space=pltpu.HBM)] * 6,
        out_specs=[vmem] * 5,
        scratch_shapes=[
            pltpu.VMEM((D, LAT), BF16),
            pltpu.VMEM((LAT, D), BF16),
            pltpu.VMEM((LAT, D), BF16),
            pltpu.VMEM((D, LAT), BF16),
            pltpu.VMEM((ROWS, LAT), jnp.int32),
            pltpu.VMEM((1, LAT), F32),
            pltpu.VMEM((1, D), F32),
            pltpu.VMEM((2, ROWS, HALF), BF16),
            pltpu.VMEM((2, HALF, ROWS), BF16),
            pltpu.VMEM((ROWS, LAT), F32),
            pltpu.VMEM((2, ROWS, QUARTER), F32),
            pltpu.VMEM((ROWS, LAT), BF16),
            pltpu.VMEM((LAT, ROWS), BF16),
            pltpu.VMEM((2, 2, ROWS, QUARTER), BF16),
            pltpu.VMEM((ROWS, LAT), BF16),
            pltpu.VMEM((2, 2, ROWS, QUARTER), BF16),
            pltpu.VMEM((2, 2, ROWS, QUARTER), BF16),
            pltpu.VMEM((2, 2, ROWS, QUARTER), BF16),
            pltpu.VMEM((2, 2, PEERS + 1, OWN, QUARTER), BF16),
            pltpu.VMEM((2, DEPTH // 2, OWN, QUARTER), BF16),
            pltpu.VMEM((PEERS + 1, D), F32),
            pltpu.VMEM((4, OWN, QUARTER), F32),
            pltpu.SemaphoreType.DMA((6,)),
            pltpu.SemaphoreType.DMA((9,)),
            pltpu.SemaphoreType.DMA((3, PEERS + 1)),
            pltpu.SemaphoreType.DMA((2, 2)),
            pltpu.SemaphoreType.DMA((2,)),
            pltpu.SemaphoreType.DMA((9,)),
            pltpu.SemaphoreType.DMA((9,)),
            pltpu.SemaphoreType.DMA((2, 3)),
            pltpu.SemaphoreType.REGULAR((3,)),
        ],
        compiler_params=pltpu.CompilerParams(
            collective_id=0, has_side_effects=True, vmem_limit_bytes=40 * 2**20
        ),
        cost_estimate=pl.CostEstimate(
            flops=10 * ROWS * D * LAT, bytes_accessed=5 * 2**20, transcendentals=0
        ),
        name="sae_backward",
    )(*(pltpu.with_memory_space_constraint(a, pltpu.HBM) for a in arrays))
    genc, geb, gdec, gdb, gin = pl.pallas_call(
        place,
        out_shape=shapes,
        in_specs=[vmem] * 5,
        out_specs=[anywhere] * 5,
        scratch_shapes=[pltpu.SemaphoreType.DMA((5,))],
        compiler_params=pltpu.CompilerParams(vmem_limit_bytes=2**18),
        name="place",
    )(*(pltpu.with_memory_space_constraint(a, pltpu.VMEM) for a in results))
    return genc, geb.reshape(LAT), gdec, gdb.reshape(D), gin


def solution(mesh):
    split = P(None, ("wide", "sub"))
    rows = P(("wide", "sub"), None)
    line = P(("wide", "sub"))
    return jax.shard_map(
        per_device,
        mesh=mesh,
        in_specs=(P("sub", None), split, line, rows, P(), split),
        out_specs=(split, line, rows, P(), P("sub", None)),
        check_vma=False,
    )
```
